32 devices in a mesh: grp: 2 (over y), fsdp: 4 (over z), rows: 4 (over x, core).
Axes of the slice: x: 2, y: 2, z: 4, core: 2. Of those that a mesh axis runs over, the one named last changes fastest.
Arguments:
- rollout: bfloat16 [4096, 8192], P(('grp', 'fsdp', 'rows')), parts along dimension 0, may hold values from -6 to 6
- row_adapter_index: int32 [4096, 1], P(('grp', 'fsdp', 'rows')), parts along dimension 0, may hold values from 0 to 15; in each aligned block of 128 rows (0 to 127, 128 to 255, ...) at most 16 rows name the same one
- frozen_key_weight: bfloat16 [8192, 1024], P('fsdp'), may hold values from -0.0625 to 0.0625
- adapter_down_weight: bfloat16 [32, 8192, 64], P(('grp', 'fsdp', 'rows')), parts along dimension 0, may hold values from -0.0625 to 0.0625
- adapter_up_weight: bfloat16 [32, 64, 1024], P(('grp', 'fsdp', 'rows')), parts along dimension 0, may hold values from -0.75 to 0.75
- output_gradient: bfloat16 [4096, 1024], P(('grp', 'fsdp', 'rows')), parts along dimension 0, may hold values from -6 to 6
Outputs:
- mixed: bfloat16 [4096, 1024], P(('grp', 'fsdp', 'rows')), parts along dimension 0
- grad_down: float32 [32, 8192, 64], P(('grp', 'fsdp', 'rows')), parts along dimension 0
- up_matrix_gradient: float32 [32, 64, 1024], P(('grp', 'fsdp', 'rows')), parts along dimension 0
The draws below stay inside these ranges and needn't reach their ends.
There are 2 independent parts, one for each index of `grp`. The reference program is written for one: setup_inputs(seed, part) draws one part's arguments, and reference() takes and returns one part's arrays. A program takes and returns all parts, laid end to end along the dimension named above; an argument that names none is the same for every part. Nothing has to cross between parts.
Inputs may be any that keep to these rules, and one draw needn't show every extreme that they name: `row_adapter_index`: in each aligned block of 128 rows (the rows of one device) no adapter is named by more than 16 rows, a bound that some block reaches.
All inputs are finite; a program needn't handle non-finite values.
Results may differ from the reference program's by a relative error of at most 0.0045.
Values may be sent and summed in bfloat16 or wider, within the bound.
No kernel may reach another device: no remote copies, remote signals or barrier semaphores. Data moves between devices by JAX's collectives and lax.ppermute only.
A program may use at most 128 MiB of HBM per device.

```python
import math
import jax
import jax.numpy as jnp
import numpy as np
from jax import lax

MODEL_WIDTH = 8192
KEY_OUTPUTS = 1024
ADAPTER_RANK = 64
TOK_DEV = 128
EXPERT_COUNT = 16
CAP = 16
TOKEN_ROWS = 2048


def block_levels(own_key, shape, shards, low, top_value):
    level, own = 1.0, jax.random.fold_in(own_key, 6)
    for position, parts in shards:
        steps = jnp.exp(jax.random.uniform(jax.random.fold_in(own, position), (parts,), jnp.float32, low / len(shards), top_value / len(shards)))
        level = level * jnp.repeat(steps, shape[position] // parts).reshape([-1 if axis == position else 1 for axis in range(len(shape))])
    return level


def deal_out(rng, own, number, rows, amount, top, bound, skew):
    ranking = jax.random.permutation(rng, amount)
    packed, usual = shares(amount, rows * top, bound, skew, True), shares(amount, rows * top, bound, skew, False)
    places = jnp.arange(amount)

    def named(tallies, turn):
        used = int((tallies > 0).sum())
        fixed = max(1, used // 4)
        shifted = fixed + (places - fixed + turn * (used - fixed)) % max(1, amount - fixed)
        return jnp.zeros((amount,), jnp.int32).at[ranking[jnp.where(places < fixed, places, shifted)]].set(jnp.asarray(tallies, jnp.int32))

    tallies = jnp.where(number % 4 == 0, named(packed, number // 4), named(usual, number - number // 4 - 1))
    mixed = jax.random.permutation(jax.random.fold_in(own, 3), amount)
    donor, sink = mixed[0:amount // 2 * 2:2], mixed[1:amount // 2 * 2:2]
    room = jnp.minimum(tallies[donor] - 1, bound - tallies[sink]) // 2
    room = jnp.where((donor == ranking[0]) | (sink == ranking[0]) | (tallies[sink] == 0), 0, jnp.maximum(room, 0))
    shifted = jax.random.randint(jax.random.fold_in(own, 4), (amount // 2,), 0, 1 << 20) % (room + 1)
    tallies = tallies.at[donor].add(-shifted).at[sink].add(shifted)
    items = jnp.searchsorted(jnp.cumsum(tallies), jnp.arange(rows * top), side="right").astype(jnp.int32)
    table = items.reshape(top, rows).T
    table = table[jax.random.permutation(jax.random.fold_in(own, 1), rows)]
    turn = jax.random.randint(jax.random.fold_in(own, 2), (rows, 1), 0, top)
    return jnp.take_along_axis(table, (jnp.arange(top)[None, :] + turn) % top, axis=1)


def shares(amount, total, most, skew, full):
    loads = [(1 << 20) // math.isqrt(rank ** skew) + 1 for rank in range(1, amount + 1)]
    largest = most if full else min(most, max(-(-total // amount), total * loads[0] // sum(loads)))
    least = 1 if total - largest >= amount - 1 else 0
    holding, spare = [largest] + [least] * (amount - 1), total - largest - least * (amount - 1)
    while spare > 0:
        movable = [i for i in range(1, amount) if holding[i] < largest] or [i for i in range(1, amount) if holding[i] < most]
        pool, budget = sum([loads[i] for i in movable]), spare
        for i in movable:
            more = min(most - holding[i], max(1, budget * loads[i] // pool), spare)
            holding[i] = holding[i] + more
            spare = spare - more
    return np.array(holding)


def bell_draw(rng, shape, scale, most, shards=(), held_as=jnp.bfloat16):
    values = scale * jax.random.normal(rng, shape, jnp.float32)
    if shards:
        values = values * block_levels(rng, shape, shards, -0.22, 0.18)
    return jnp.clip(values, -most, most).astype(held_as)


def setup_inputs(seed: int = 0, part: int = 0) -> dict:
    keys = jax.random.split(jax.random.key(seed), 7)
    part_splits = jax.random.split(jax.random.fold_in(keys[6], part), 7)
    rollout = bell_draw(part_splits[0], (TOKEN_ROWS, MODEL_WIDTH), 1.0, 6.0, ((0, 16),))
    row_adapter_index_keys = jax.random.split(jax.random.fold_in(part_splits[1], 1), TOKEN_ROWS // TOK_DEV)
    row_adapter_index_turns = jax.random.permutation(jax.random.fold_in(part_splits[1], 3), TOKEN_ROWS // TOK_DEV)
    row_adapter_index = jax.vmap(lambda own, number: deal_out(jax.random.fold_in(part_splits[1], 2), own, number, TOK_DEV, EXPERT_COUNT, 1, CAP, 2))(row_adapter_index_keys, row_adapter_index_turns).reshape((TOKEN_ROWS, 1))
    frozen_key_weight = bell_draw(keys[2], (MODEL_WIDTH, KEY_OUTPUTS), MODEL_WIDTH ** -0.5, 0.0625, ((0, 4),))
    adapter_down_weight = bell_draw(part_splits[3], (EXPERT_COUNT, MODEL_WIDTH, ADAPTER_RANK), MODEL_WIDTH ** -0.5, 0.0625, ((0, 16),))
    adapter_up_weight = bell_draw(part_splits[4], (EXPERT_COUNT, ADAPTER_RANK, KEY_OUTPUTS), ADAPTER_RANK ** -0.5, 0.75, ((0, 16),))
    output_gradient = bell_draw(part_splits[5], (TOKEN_ROWS, KEY_OUTPUTS), 1.0, 6.0, ((0, 16),))
    return dict(rollout=rollout, row_adapter_index=row_adapter_index, frozen_key_weight=frozen_key_weight, adapter_down_weight=adapter_down_weight, adapter_up_weight=adapter_up_weight, output_gradient=output_gradient)


adapter_scale = 0.5


def reference(rollout, row_adapter_index, frozen_key_weight, adapter_down_weight, adapter_up_weight, output_gradient):
    ids = row_adapter_index[:, 0]
    frozen_output = jnp.dot(rollout, frozen_key_weight, preferred_element_type=jnp.float32)
    x_pad = jnp.concatenate([rollout, jnp.zeros((1, MODEL_WIDTH), rollout.dtype)], 0)
    dy_pad = jnp.concatenate([output_gradient, jnp.zeros((1, KEY_OUTPUTS), output_gradient.dtype)], 0)

    def one_adapter(adapter_index):
        matched_rows = jnp.nonzero(ids == adapter_index, size=2 * TOK_DEV, fill_value=TOKEN_ROWS)[0].astype(jnp.int32)
        x_rows = x_pad[matched_rows]
        gradient_rows = dy_pad[matched_rows]
        down_matrix = adapter_down_weight[adapter_index]
        up_matrix = adapter_up_weight[adapter_index]
        hidden_state = jnp.dot(x_rows, down_matrix, preferred_element_type=jnp.float32).astype(jnp.bfloat16)
        adapter_term = (adapter_scale * jnp.dot(hidden_state, up_matrix, preferred_element_type=jnp.float32)).astype(jnp.bfloat16)
        returned_rows = (adapter_scale * lax.dot_general(gradient_rows, up_matrix, (((1,), (1,)), ((), ())), preferred_element_type=jnp.float32)).astype(jnp.bfloat16)
        up_gradient_local = adapter_scale * lax.dot_general(hidden_state, gradient_rows, (((0,), (0,)), ((), ())), preferred_element_type=jnp.float32)
        g_down = lax.dot_general(x_rows, returned_rows, (((0,), (0,)), ((), ())), preferred_element_type=jnp.float32)
        return matched_rows, adapter_term, g_down, up_gradient_local

    matched_rows, adapter_terms, grad_down, up_matrix_gradient = lax.map(one_adapter, jnp.arange(EXPERT_COUNT, dtype=jnp.int32))
    adapter_row_output = jnp.zeros((TOKEN_ROWS + 1, KEY_OUTPUTS), jnp.bfloat16).at[matched_rows.reshape(-1)].set(adapter_terms.reshape(-1, KEY_OUTPUTS))[:TOKEN_ROWS]
    mixed = (frozen_output + adapter_row_output.astype(jnp.float32)).astype(jnp.bfloat16)
    return mixed, grad_down, up_matrix_gradient
```

```python
import jax
import jax.numpy as jnp
from jax import lax
from jax.sharding import PartitionSpec as P

adapter_scale = 0.5
chunks = 2
bf16, f32 = jnp.bfloat16, jnp.float32


def swap(a, axis, bits):
    n = lax.axis_size(axis)
    return lax.ppermute(a, axis, [(i, i ^ bits) for i in range(n)])


def gather(a, axis):
    held = a[None]
    bit = lax.axis_size(axis) // 2
    while bit:
        got = swap(held, axis, bit)
        held = jnp.stack([held, got], 1).reshape((-1,) + a.shape)
        bit //= 2
    return held


def exchange(pieces, axis):
    return [p if m == 0 else swap(p, axis, m) for m, p in enumerate(pieces)]


def scatter(even, odd, axis):
    bit = 1
    while True:
        even = even + swap(odd, axis, bit).astype(f32)
        bit *= 2
        if bit == lax.axis_size(axis):
            return even[0]
        pairs = even.reshape((even.shape[0] // 2, 2) + even.shape[1:])
        even, odd = pairs[:, 0], pairs[:, 1].astype(bf16)


def scatter_all(a, axis):
    pairs = a.reshape((a.shape[0] // 2, 2) + a.shape[1:])
    return scatter(pairs[:, 0], pairs[:, 1].astype(bf16), axis)


def cut(a, size, start):
    n_f = lax.axis_size("fsdp")
    depth = a.shape[1] // n_f
    f = lax.axis_index("fsdp")
    return [
        lax.dynamic_slice_in_dim(a, (f ^ n) * depth + start, size, 1) for n in range(n_f)
    ]


def dot(a, b, da, db):
    return lax.dot_general(a, b, (((da,), (db,)), ((), ())), preferred_element_type=f32)


def pick(wide, row_ids, column_ids):
    wide = wide.reshape(wide.shape[0], column_ids.shape[0], -1)
    mask = row_ids[:, None] == column_ids[None, :]
    return jnp.sum(jnp.where(mask[:, :, None], wide, 0.0), 1)


def spread(narrow, row_ids, column_ids):
    mask = row_ids[:, None] == column_ids[None, :]
    wide = jnp.where(mask[:, :, None], narrow[:, None, :], jnp.zeros((), narrow.dtype))
    return wide.reshape(narrow.shape[0], -1)


def per_device(
    rollout,
    row_adapter_index,
    frozen_key_weight,
    adapter_down_weight,
    adapter_up_weight,
    output_gradient,
):
    count, width = rollout.shape
    n_f = lax.axis_size("fsdp")
    n_r = lax.axis_size("rows")
    f = lax.axis_index("fsdp")
    r = lax.axis_index("rows")
    depth = width // n_f
    part = depth // chunks
    rank = adapter_down_weight.shape[2]
    outputs = frozen_key_weight.shape[1]
    owners = n_r * n_f

    ids = row_adapter_index[:, 0]
    down_t = jnp.swapaxes(adapter_down_weight[0], 0, 1)
    up = adapter_up_weight[0]

    ms = jnp.arange(n_r, dtype=jnp.int32)
    ns = jnp.arange(n_f, dtype=jnp.int32)
    adapters = (f ^ ns)[None, :] * n_r + (r ^ ms)[:, None]
    all_ids = adapters.reshape(-1)
    even_ids = adapters[0::2].reshape(-1)
    odd_ids = adapters[1::2].reshape(-1)

    up_own = gather(up, "fsdp")
    down_pieces = exchange(cut(down_t, depth, 0), "fsdp")
    down_own = jnp.stack(down_pieces)
    up_all = gather(up_own, "rows").reshape(owners * rank, outputs)
    down_all = gather(down_own, "rows").reshape(owners * rank, depth)

    back = (adapter_scale * pick(dot(output_gradient, up_all, 1, 1), ids, all_ids)).astype(bf16)
    packed = jnp.concatenate(
        [back, jnp.broadcast_to(ids[:, None].astype(bf16), (count, rank))], 1
    )
    packed = jnp.concatenate(exchange([packed] * n_f, "fsdp"), 0)
    back_rows = packed[:, :rank]
    row_ids = packed[:, rank].astype(jnp.int32)
    back_even = spread(back_rows, row_ids, even_ids)
    back_odd = spread(back_rows, row_ids, odd_ids)

    group = owners
    while group * rank * row_ids.shape[0] > 1 << 21 and group % 2 == 0:
        group //= 2

    def hidden_of(x_part, down_part):
        if group == owners:
            return pick(dot(x_part, down_part, 1, 1), row_ids, all_ids)

        def one(g, total):
            down = lax.dynamic_slice_in_dim(down_part, g * group * rank, group * rank, 0)
            names = lax.dynamic_slice_in_dim(all_ids, g * group, group, 0)
            return total + pick(dot(x_part, down, 1, 1), row_ids, names)

        return lax.fori_loop(
            0, owners // group, one, jnp.zeros((row_ids.shape[0], rank), f32)
        )

    base = 0.0
    hidden_part = 0.0
    grad_pieces = []
    for c in range(chunks):
        x_pieces = exchange(cut(rollout, part, c * part), "fsdp")
        x_part = jnp.concatenate(x_pieces, 0)
        odd = dot(back_odd, x_part, 0, 0).astype(bf16).reshape(n_r // 2, n_f * rank, part)
        even = dot(back_even, x_part, 0, 0).reshape(n_r // 2, n_f * rank, part)
        grad_pieces.append(scatter(even, odd, "rows"))
        span = slice(c * part, (c + 1) * part)
        base = base + dot(x_part, frozen_key_weight[span], 1, 0)
        hidden_part = hidden_part + hidden_of(x_part, down_all[:, span])

    hidden = exchange(list(hidden_part.reshape(n_f, count, rank)), "fsdp")
    hidden = sum(hidden[1:], hidden[0]).astype(bf16)
    lora = (adapter_scale * dot(spread(hidden, ids, all_ids), up_all, 1, 0)).astype(bf16)
    total = scatter_all(base.reshape(n_f, count, outputs), "fsdp")
    mixed = (total + lora.astype(f32)).astype(bf16)

    odd = adapter_scale * dot(spread(hidden, ids, odd_ids), output_gradient, 0, 0)
    even = adapter_scale * dot(spread(hidden, ids, even_ids), output_gradient, 0, 0)
    up_grad = scatter(
        even.reshape(n_r // 2, n_f * rank, outputs),
        odd.astype(bf16).reshape(n_r // 2, n_f * rank, outputs),
        "rows",
    )
    up_grad = scatter_all(up_grad.reshape(n_f, rank, outputs), "fsdp")

    grad_down = jnp.zeros((rank, width), f32)
    for c in range(chunks):
        piece = grad_pieces[c].reshape(n_f, rank, part)
        got = exchange([piece[0]] + [piece[n].astype(bf16) for n in range(1, n_f)], "fsdp")
        for n in range(n_f):
            at = (f ^ n) * depth + c * part
            grad_down = lax.dynamic_update_slice_in_dim(grad_down, got[n].astype(f32), at, 1)
    return (mixed, jnp.swapaxes(grad_down, 0, 1)[None], up_grad[None])


def solution(mesh):
    return jax.shard_map(
        per_device,
        mesh=mesh,
        in_specs=(
            P(("grp", "fsdp", "rows"), None),
            P(("grp", "fsdp", "rows"), None),
            P("fsdp", None),
            P(("grp", "fsdp", "rows"), None, None),
            P(("grp", "fsdp", "rows"), None, None),
            P(("grp", "fsdp", "rows"), None),
        ),
        out_specs=(
            P(("grp", "fsdp", "rows"), None),
            P(("grp", "fsdp", "rows"), None, None),
            P(("grp", "fsdp", "rows"), None, None),
        ),
        check_vma=False,
    )
```

```python
import jax
import jax.numpy as jnp
from jax import lax
from jax.experimental import pallas as pl
from jax.experimental.pallas import tpu as pltpu
from jax.sharding import PartitionSpec as P

adapter_scale = 0.5
chunks = 2
bf16, f32 = jnp.bfloat16, jnp.float32


def swap(a, axis, bits):
    n = lax.axis_size(axis)
    return lax.ppermute(a, axis, [(i, i ^ bits) for i in range(n)])


def gather(a, axis, first=None):
    held = a[None]
    bit = lax.axis_size(axis) // 2
    while bit:
        got = swap(held, axis, bit) if first is None or held.shape[0] > 1 else first
        if held.shape[0] == 1:
            first = got
        held = jnp.stack([held, got], 1).reshape((-1,) + a.shape)
        bit //= 2
    return held, first, got


def exchange(pieces, axis):
    return [p if m == 0 else swap(p, axis, m) for m, p in enumerate(pieces)]


def scatter(even, odd, axis):
    bit = 1
    while True:
        even = even + swap(odd, axis, bit).astype(f32)
        bit *= 2
        if bit == lax.axis_size(axis):
            return even[0]
        pairs = even.reshape((even.shape[0] // 2, 2) + even.shape[1:])
        even, odd = pairs[:, 0], pairs[:, 1].astype(bf16)


def scatter_all(a, axis):
    pairs = a.reshape((a.shape[0] // 2, 2) + a.shape[1:])
    return scatter(pairs[:, 0], pairs[:, 1].astype(bf16), axis)


any_space = pl.BlockSpec(memory_space=pl.ANY)
hbm_space = pl.BlockSpec(memory_space=pltpu.HBM)


def cut(a, size, start, *others):
    n_f = lax.axis_size("fsdp")
    depth = a.shape[1] // n_f

    def body(index, source, *refs):
        outs, (held, sem_in, sem_out) = refs[len(others) : -3], refs[-3:]
        loads, stores = [], []
        for n in range(n_f):
            at = pl.multiple_of((index[0] ^ n) * depth + start, 128)
            loads.append(
                pltpu.make_async_copy(source.at[:, pl.ds(at, size)], held.at[n], sem_in.at[n])
            )
            stores.append(pltpu.make_async_copy(held.at[n], outs[n], sem_out.at[n]))
        for load in loads:
            load.start()
        for load, store in zip(loads, stores):
            load.wait()
            store.start()
        for store in stores:
            store.wait()

    return pl.pallas_call(
        body,
        out_shape=[jax.ShapeDtypeStruct((a.shape[0], size), a.dtype)] * n_f,
        in_specs=[pl.BlockSpec(memory_space=pltpu.SMEM)] + [any_space] + [hbm_space] * len(others),
        out_specs=[any_space] * n_f,
        scratch_shapes=[
            pltpu.VMEM((n_f, a.shape[0], size), a.dtype),
            pltpu.SemaphoreType.DMA((n_f,)),
            pltpu.SemaphoreType.DMA((n_f,)),
        ],
        cost_estimate=pl.CostEstimate(
            flops=0, bytes_accessed=2 * n_f * a.shape[0] * size * 2, transcendentals=0
        ),
    )(lax.axis_index("fsdp")[None], a, *others)


def copied(a, *others):
    flat = a.reshape(-1, a.shape[-1])
    rows = min(512, flat.shape[0])

    def body(source, *refs):
        refs[-1][...] = source[...]

    block = pl.BlockSpec((rows, flat.shape[1]), lambda i: (i, 0))
    return pl.pallas_call(
        body,
        grid=(flat.shape[0] // rows,),
        out_shape=jax.ShapeDtypeStruct(flat.shape, a.dtype),
        in_specs=[block] + [hbm_space] * len(others),
        out_specs=block,
        cost_estimate=pl.CostEstimate(
            flops=0, bytes_accessed=4 * a.size, transcendentals=0
        ),
    )(flat, *others).reshape(a.shape)


def dot(a, b, da, db):
    return lax.dot_general(a, b, (((da,), (db,)), ((), ())), preferred_element_type=f32)


def pick(wide, row_ids, column_ids):
    wide = wide.reshape(wide.shape[0], column_ids.shape[0], -1)
    mask = row_ids[:, None] == column_ids[None, :]
    return jnp.sum(jnp.where(mask[:, :, None], wide, 0.0), 1)


def spread(narrow, row_ids, column_ids):
    mask = row_ids[:, None] == column_ids[None, :]
    wide = jnp.where(mask[:, :, None], narrow[:, None, :], jnp.zeros((), narrow.dtype))
    return wide.reshape(narrow.shape[0], -1)


def per_device(
    rollout,
    row_adapter_index,
    frozen_key_weight,
    adapter_down_weight,
    adapter_up_weight,
    output_gradient,
):
    count, width = rollout.shape
    n_f = lax.axis_size("fsdp")
    n_r = lax.axis_size("rows")
    f = lax.axis_index("fsdp")
    r = lax.axis_index("rows")
    depth = width // n_f
    part = depth // chunks
    rank = adapter_down_weight.shape[2]
    outputs = frozen_key_weight.shape[1]
    owners = n_r * n_f

    ids = row_adapter_index[:, 0]
    down_t = jnp.swapaxes(adapter_down_weight[0], 0, 1)
    up = adapter_up_weight[0]

    ms = jnp.arange(n_r, dtype=jnp.int32)
    ns = jnp.arange(n_f, dtype=jnp.int32)
    adapters = (f ^ ns)[None, :] * n_r + (r ^ ms)[:, None]
    all_ids = adapters.reshape(-1)
    even_ids = adapters[0::2].reshape(-1)
    odd_ids = adapters[1::2].reshape(-1)

    up_first = swap(up[None], "fsdp", n_f // 2)
    up_own, _, _ = gather(up, "fsdp", up_first)
    up_all, up_across, up_last = gather(up_own, "rows")
    up_all = up_all.reshape(owners * rank, outputs)
    down_pieces = exchange(cut(down_t, depth, 0, up_first), "fsdp")
    down_own = jnp.stack(down_pieces)
    down_all, _, _ = gather(down_own, "rows")
    down_all = down_all.reshape(owners * rank, depth)

    back = (adapter_scale * pick(dot(output_gradient, up_all, 1, 1), ids, all_ids)).astype(bf16)
    packed = jnp.concatenate(
        [back, jnp.broadcast_to(ids[:, None].astype(bf16), (count, rank))], 1
    )
    packed = jnp.concatenate(exchange([packed] * n_f, "fsdp"), 0)
    back_rows = packed[:, :rank]
    row_ids = packed[:, rank].astype(jnp.int32)
    back_even = spread(back_rows, row_ids, even_ids)
    back_odd = spread(back_rows, row_ids, odd_ids)

    group = owners
    while group * rank * row_ids.shape[0] > 1 << 21 and group % 2 == 0:
        group //= 2

    def hidden_of(x_part, down_part):
        if group == owners:
            return pick(dot(x_part, down_part, 1, 1), row_ids, all_ids)

        def one(g, total):
            down = lax.dynamic_slice_in_dim(down_part, g * group * rank, group * rank, 0)
            names = lax.dynamic_slice_in_dim(all_ids, g * group, group, 0)
            return total + pick(dot(x_part, down, 1, 1), row_ids, names)

        return lax.fori_loop(
            0, owners // group, one, jnp.zeros((row_ids.shape[0], rank), f32)
        )

    base = 0.0
    hidden_part = 0.0
    grad_pieces = []
    cut_after = [(down_pieces[n_f // 2],), ()]
    for c in range(chunks):
        x_pieces = exchange(cut(rollout, part, c * part, *cut_after[c]), "fsdp")
        if c + 1 < chunks:
            cut_after[c + 1] += (x_pieces[n_f // 2],)
        x_part = jnp.concatenate(x_pieces, 0)
        odd = dot(back_odd, x_part, 0, 0).astype(bf16).reshape(n_r // 2, n_f * rank, part)
        even = dot(back_even, x_part, 0, 0).reshape(n_r // 2, n_f * rank, part)
        grad_pieces.append(scatter(even, odd, "rows"))
        span = slice(c * part, (c + 1) * part)
        base = base + dot(x_part, frozen_key_weight[span], 1, 0)
        hidden_part = hidden_part + hidden_of(x_part, down_all[:, span])

    hidden = exchange(list(hidden_part.reshape(n_f, count, rank)), "fsdp")
    hidden = sum(hidden[1:], hidden[0]).astype(bf16)
    lora = (adapter_scale * dot(spread(hidden, ids, all_ids), up_all, 1, 0)).astype(bf16)
    total = scatter_all(base.reshape(n_f, count, outputs), "fsdp")
    mixed = (total + lora.astype(f32)).astype(bf16)

    odd = adapter_scale * dot(spread(hidden, ids, odd_ids), output_gradient, 0, 0)
    even = adapter_scale * dot(spread(hidden, ids, even_ids), output_gradient, 0, 0)
    up_grad = scatter(
        even.reshape(n_r // 2, n_f * rank, outputs),
        odd.astype(bf16).reshape(n_r // 2, n_f * rank, outputs),
        "rows",
    )
    down_moved = []
    for c in range(chunks):
        piece = grad_pieces[c].reshape(n_f, rank, part)
        down_moved.append(
            exchange([piece[0]] + [piece[n].astype(bf16) for n in range(1, n_f)], "fsdp")
        )
    grad_down = jnp.zeros((rank, width), f32)
    for c in range(chunks):
        for n in range(n_f):
            at = (f ^ n) * depth + c * part
            got = down_moved[c][n].astype(f32)
            grad_down = lax.dynamic_update_slice_in_dim(grad_down, got, at, 1)
    pairs = up_grad.reshape(n_f // 2, 2, rank, outputs)
    odd = copied(pairs[:, 1].astype(bf16), down_moved[0][n_f // 2])
    up_grad = scatter(pairs[:, 0], odd, "fsdp")

    return (mixed, jnp.swapaxes(grad_down, 0, 1)[None], up_grad[None])


def solution(mesh):
    return jax.shard_map(
        per_device,
        mesh=mesh,
        in_specs=(
            P(("grp", "fsdp", "rows"), None),
            P(("grp", "fsdp", "rows"), None),
            P("fsdp", None),
            P(("grp", "fsdp", "rows"), None, None),
            P(("grp", "fsdp", "rows"), None, None),
            P(("grp", "fsdp", "rows"), None),
        ),
        out_specs=(
            P(("grp", "fsdp", "rows"), None),
            P(("grp", "fsdp", "rows"), None, None),
            P(("grp", "fsdp", "rows"), None, None),
        ),
        check_vma=False,
    )
```

```python
import jax
import jax.numpy as jnp
from jax import lax
from jax.experimental import pallas as pl
from jax.experimental.pallas import tpu as pltpu
from jax.sharding import PartitionSpec as P

adapter_scale = 0.5
chunks = 2
bf16, f32 = jnp.bfloat16, jnp.float32


def swap(a, axis, bits):
    n = lax.axis_size(axis)
    return lax.ppermute(a, axis, [(i, i ^ bits) for i in range(n)])


def gather(a, axis, first=None):
    held = a[None]
    bit = lax.axis_size(axis) // 2
    while bit:
        got = swap(held, axis, bit) if first is None or held.shape[0] > 1 else first
        if held.shape[0] == 1:
            first = got
        held = jnp.stack([held, got], 1).reshape((-1,) + a.shape)
        bit //= 2
    return held, first, got


def exchange(pieces, axis):
    return [p if m == 0 else swap(p, axis, m) for m, p in enumerate(pieces)]


def scatter(even, odd, axis):
    bit = 1
    while True:
        even = even + swap(odd, axis, bit).astype(f32)
        bit *= 2
        if bit == lax.axis_size(axis):
            return even[0]
        pairs = even.reshape((even.shape[0] // 2, 2) + even.shape[1:])
        even, odd = pairs[:, 0], pairs[:, 1].astype(bf16)


def scatter_all(a, axis):
    pairs = a.reshape((a.shape[0] // 2, 2) + a.shape[1:])
    return scatter(pairs[:, 0], pairs[:, 1].astype(bf16), axis)


any_space = pl.BlockSpec(memory_space=pl.ANY)
hbm_space = pl.BlockSpec(memory_space=pltpu.HBM)


def cut(a, size, start, *others):
    n_f = lax.axis_size("fsdp")
    depth = a.shape[1] // n_f

    def body(index, source, *refs):
        outs, (held, sem_in, sem_out) = refs[len(others) : -3], refs[-3:]
        loads, stores = [], []
        for n in range(n_f):
            at = pl.multiple_of((index[0] ^ n) * depth + start, 128)
            loads.append(
                pltpu.make_async_copy(source.at[:, pl.ds(at, size)], held.at[n], sem_in.at[n])
            )
            stores.append(pltpu.make_async_copy(held.at[n], outs[n], sem_out.at[n]))
        for load in loads:
            load.start()
        for load, store in zip(loads, stores):
            load.wait()
            store.start()
        for store in stores:
            store.wait()

    return pl.pallas_call(
        body,
        out_shape=[jax.ShapeDtypeStruct((a.shape[0], size), a.dtype)] * n_f,
        in_specs=[pl.BlockSpec(memory_space=pltpu.SMEM)] + [any_space] + [hbm_space] * len(others),
        out_specs=[any_space] * n_f,
        scratch_shapes=[
            pltpu.VMEM((n_f, a.shape[0], size), a.dtype),
            pltpu.SemaphoreType.DMA((n_f,)),
            pltpu.SemaphoreType.DMA((n_f,)),
        ],
        cost_estimate=pl.CostEstimate(
            flops=0, bytes_accessed=2 * n_f * a.shape[0] * size * 2, transcendentals=0
        ),
    )(lax.axis_index("fsdp")[None], a, *others)


def copied(a, *others):
    flat = a.reshape(-1, a.shape[-1])
    rows = min(512, flat.shape[0])

    def body(source, *refs):
        refs[-1][...] = source[...]

    block = pl.BlockSpec((rows, flat.shape[1]), lambda i: (i, 0))
    return pl.pallas_call(
        body,
        grid=(flat.shape[0] // rows,),
        out_shape=jax.ShapeDtypeStruct(flat.shape, a.dtype),
        in_specs=[block] + [hbm_space] * len(others),
        out_specs=block,
        cost_estimate=pl.CostEstimate(
            flops=0, bytes_accessed=4 * a.size, transcendentals=0
        ),
    )(flat, *others).reshape(a.shape)


def dot(a, b, da, db):
    return lax.dot_general(a, b, (((da,), (db,)), ((), ())), preferred_element_type=f32)


def pick(wide, row_ids, column_ids):
    wide = wide.reshape(wide.shape[0], column_ids.shape[0], -1)
    mask = row_ids[:, None] == column_ids[None, :]
    return jnp.sum(jnp.where(mask[:, :, None], wide, 0.0), 1)


def spread(narrow, row_ids, column_ids):
    mask = row_ids[:, None] == column_ids[None, :]
    wide = jnp.where(mask[:, :, None], narrow[:, None, :], jnp.zeros((), narrow.dtype))
    return wide.reshape(narrow.shape[0], -1)


def per_device(
    rollout,
    row_adapter_index,
    frozen_key_weight,
    adapter_down_weight,
    adapter_up_weight,
    output_gradient,
):
    count, width = rollout.shape
    n_f = lax.axis_size("fsdp")
    n_r = lax.axis_size("rows")
    f = lax.axis_index("fsdp")
    r = lax.axis_index("rows")
    depth = width // n_f
    part = depth // chunks
    rank = adapter_down_weight.shape[2]
    outputs = frozen_key_weight.shape[1]
    owners = n_r * n_f

    ids = row_adapter_index[:, 0]
    down_t = jnp.swapaxes(adapter_down_weight[0], 0, 1)
    up = adapter_up_weight[0]

    ms = jnp.arange(n_r, dtype=jnp.int32)
    ns = jnp.arange(n_f, dtype=jnp.int32)
    adapters = (f ^ ns)[None, :] * n_r + (r ^ ms)[:, None]
    all_ids = adapters.reshape(-1)
    even_ids = adapters[0::2].reshape(-1)
    odd_ids = adapters[1::2].reshape(-1)

    up_first = swap(up[None], "fsdp", n_f // 2)
    up_own, _, _ = gather(up, "fsdp", up_first)
    up_all, _, _ = gather(up_own, "rows")
    up_all = up_all.reshape(owners * rank, outputs)
    down_pieces = exchange(cut(down_t, depth, 0, up_first), "fsdp")
    down_own = jnp.stack(down_pieces)
    held, bit = down_own[None], n_r // 2
    while bit > 1:
        got = swap(held, "rows", bit)
        held = jnp.stack([held, got], 1).reshape((-1,) + down_own.shape)
        bit //= 2
    downs = [
        h.reshape(owners // 2 * rank, depth) for h in (held, swap(held, "rows", 1))
    ]

    back = (adapter_scale * pick(dot(output_gradient, up_all, 1, 1), ids, all_ids)).astype(bf16)
    packed = jnp.concatenate(
        [back, jnp.broadcast_to(ids[:, None].astype(bf16), (count, rank))], 1
    )
    packed = jnp.concatenate(exchange([packed] * n_f, "fsdp"), 0)
    back_rows = packed[:, :rank]
    row_ids = packed[:, rank].astype(jnp.int32)
    back_even = spread(back_rows, row_ids, even_ids)
    back_odd = spread(back_rows, row_ids, odd_ids)

    group = owners // 2
    while group * rank * row_ids.shape[0] > 1 << 20 and group % 2 == 0:
        group //= 2

    def hidden_of(x_part, down_part, names):
        if group == owners // 2:
            return pick(dot(x_part, down_part, 1, 1), row_ids, names)

        def one(g, total):
            down = lax.dynamic_slice_in_dim(down_part, g * group * rank, group * rank, 0)
            some = lax.dynamic_slice_in_dim(names, g * group, group, 0)
            return total + pick(dot(x_part, down, 1, 1), row_ids, some)

        return lax.fori_loop(
            0, owners // 2 // group, one, jnp.zeros((row_ids.shape[0], rank), f32)
        )

    base = 0.0
    hidden_part = 0.0
    grad_pieces = []
    cut_after = [(down_pieces[n_f // 2],), ()]
    for c in range(chunks):
        x_pieces = exchange(cut(rollout, part, c * part, *cut_after[c]), "fsdp")
        if c + 1 < chunks:
            cut_after[c + 1] += (x_pieces[n_f // 2],)
        x_part = jnp.concatenate(x_pieces, 0)
        odd = dot(back_odd, x_part, 0, 0).astype(bf16).reshape(n_r // 2, n_f * rank, part)
        even = dot(back_even, x_part, 0, 0).reshape(n_r // 2, n_f * rank, part)
        grad_pieces.append(scatter(even, odd, "rows"))
        span = slice(c * part, (c + 1) * part)
        base = base + dot(x_part, frozen_key_weight[span], 1, 0)
        for d, h in zip(downs, (even_ids, odd_ids)):
            hidden_part = hidden_part + hidden_of(x_part, d[:, span], h)

    hidden = exchange(list(hidden_part.reshape(n_f, count, rank)), "fsdp")
    hidden = sum(hidden[1:], hidden[0]).astype(bf16)
    lora = (adapter_scale * dot(spread(hidden, ids, all_ids), up_all, 1, 0)).astype(bf16)
    total = scatter_all(base.reshape(n_f, count, outputs), "fsdp")
    mixed = (total + lora.astype(f32)).astype(bf16)

    odd = adapter_scale * dot(spread(hidden, ids, odd_ids), output_gradient, 0, 0)
    even = adapter_scale * dot(spread(hidden, ids, even_ids), output_gradient, 0, 0)
    up_grad = scatter(
        even.reshape(n_r // 2, n_f * rank, outputs),
        odd.astype(bf16).reshape(n_r // 2, n_f * rank, outputs),
        "rows",
    )
    down_moved = []
    for c in range(chunks):
        piece = grad_pieces[c].reshape(n_f, rank, part)
        down_moved.append(
            exchange([piece[0]] + [piece[n].astype(bf16) for n in range(1, n_f)], "fsdp")
        )
    grad_down = jnp.zeros((rank, width), f32)
    for c in range(chunks):
        for n in range(n_f):
            at = (f ^ n) * depth + c * part
            got = down_moved[c][n].astype(f32)
            grad_down = lax.dynamic_update_slice_in_dim(grad_down, got, at, 1)
    pairs = up_grad.reshape(n_f // 2, 2, rank, outputs)
    odd = copied(pairs[:, 1].astype(bf16), down_moved[0][1])
    up_grad = scatter(pairs[:, 0], odd, "fsdp")

    return (mixed, jnp.swapaxes(grad_down, 0, 1)[None], up_grad[None])


def solution(mesh):
    return jax.shard_map(
        per_device,
        mesh=mesh,
        in_specs=(
            P(("grp", "fsdp", "rows"), None),
            P(("grp", "fsdp", "rows"), None),
            P("fsdp", None),
            P(("grp", "fsdp", "rows"), None, None),
            P(("grp", "fsdp", "rows"), None, None),
            P(("grp", "fsdp", "rows"), None),
        ),
        out_specs=(
            P(("grp", "fsdp", "rows"), None),
            P(("grp", "fsdp", "rows"), None, None),
            P(("grp", "fsdp", "rows"), None, None),
        ),
        check_vma=False,
    )
```
